32 devices in a mesh: groups: 2 (over y), sub: 4 (over z), coarse: 2 (over x), rep: 2 (over core).
Axes of the slice: x: 2, y: 2, z: 4, core: 2. Of those that a mesh axis runs over, the one named last changes fastest.
Arguments:
- residual: float32 [8, 2, 19200], P('rep', None, ('groups', 'sub', 'coarse')), parts along dimension 2, may hold values from -24 to 24
- elem_inv: bfloat16 [16, 720000], P(('groups', 'sub', 'coarse')), parts along dimension 0, may hold values from -2 to 2.5
- elem_faces: int32 [256, 6], P(('groups', 'sub', 'coarse')), parts along dimension 0, may hold values from -1 to 79, as said below
- send_faces: int32 [16, 4, 8], P(('groups', 'sub', 'coarse')), parts along dimension 0, may hold values from -1 to 47, as said below
- coarse_basis: bfloat16 [2, 1024, 1200], P(None, ('groups', 'sub', 'coarse')), parts along dimension 1, may hold values from -0.29882812 to 0.29882812
- coarse_inv: bfloat16 [2, 1024, 512], P(None, ('groups', 'sub', 'coarse', 'rep')), parts along dimension 1, may hold values from -0.05 to 0.05, as said below
Outputs:
- precond: float32 [8, 2, 19200], P('rep', None, ('groups', 'sub', 'coarse')), parts along dimension 2
- inner: float32 [16, 2], P(('groups', 'rep')), parts along dimension 0
The draws below stay inside these ranges and needn't reach their ends.
There are 2 independent parts, one for each index of `groups`. The reference program is written for one: setup_inputs(seed, part) draws one part's arguments, and reference() takes and returns one part's arrays. A program takes and returns all parts, laid end to end along the dimension named above; each array names one. Nothing has to cross between parts.
Inputs may be any that keep to these rules, and one draw needn't show every extreme that they name: `send_faces`: entries 0 or more are distinct within one subdomain. Slot j of subdomain s lists the faces read by subdomain s - o_j, o = (-2, -1, 1, 2), as many as that subdomain's halo slots with live entries; -1 marks an empty slot. For every subdomain s >= 2, slot 3 is full. `elem_faces`: values 48 + j * 8 + c name received faces; every live received face of a subdomain appears exactly once, every owned face once or twice; -1 is a boundary slot. Complex symmetric: coarse_inv[c, i, k] equals coarse_inv[c, k, i].
All inputs are finite; a program needn't handle non-finite values.
Results may differ from the reference program's by a relative error of at most 0.0003.
The reference program's roundings to bfloat16 on the way count: a program that leaves them out, or rounds other values in their place, can miss the bound.
Values may be sent and summed in bfloat16 or wider, within the bound.
A program may use at most 64 MiB of HBM per device.

```python
import math
import jax
import jax.numpy as jnp
from jax import lax

E_DEV = 16
FACE_DOF = 25
SOURCES = 8
NCOARSE = 64
F_DEV = 48
CAP = 8
ELEM_DOF = 150
SUBDOMAINS = 8
NCT = 512
TRACES = 9600


def counts_table(key):
    key = jax.random.fold_in(key, 11)
    raw = jax.random.randint(key, (SUBDOMAINS, 4), 1, CAP + 1, dtype=jnp.int32)
    ident = jnp.arange(SUBDOMAINS, dtype=jnp.int32)[:, None]
    offsets = jnp.array([-2, -1, 1, 2], jnp.int32)[None, :]
    source = ident + offsets
    valid = (source >= 0) & (source < SUBDOMAINS)
    column = jnp.arange(4, dtype=jnp.int32)[None, :]
    raw = jnp.where(column == 3, CAP, raw)
    return (jnp.where(valid, raw, 0), offsets)


def partition(key):
    counts, offsets = counts_table(key)
    ident = jnp.arange(SUBDOMAINS, dtype=jnp.int32)[:, None]
    dest = ident - offsets
    okay = (dest >= 0) & (dest < SUBDOMAINS)
    column = jnp.arange(4, dtype=jnp.int32)[None, :]
    outgoing_counts = jnp.where(okay, counts[jnp.clip(dest, 0, SUBDOMAINS - 1), column], 0)
    perm_keys = jax.random.split(jax.random.fold_in(key, 12), SUBDOMAINS)
    perms = jax.vmap(lambda k: jax.random.permutation(k, F_DEV))(perm_keys).astype(jnp.int32)
    chosen = perms[:, :4 * CAP].reshape(SUBDOMAINS, 4, CAP)
    slots = jnp.arange(CAP, dtype=jnp.int32)
    live = slots[None, None, :] < outgoing_counts[:, :, None]
    send = jnp.where(live, chosen, -1)
    facelist = jnp.arange(F_DEV, dtype=jnp.int32)
    sent_flag = jnp.any((chosen.reshape(SUBDOMAINS, 4 * CAP, 1) == facelist[None, None, :]) & live.reshape(SUBDOMAINS, 4 * CAP, 1), axis=1)
    halo_ids = F_DEV + jnp.arange(4 * CAP, dtype=jnp.int32).reshape(1, 4, CAP)
    halo_live = slots[None, None, :] < counts[:, :, None]
    halo_ids = jnp.where(halo_live, halo_ids, -1).reshape(SUBDOMAINS, 4 * CAP)
    owned_ids = jnp.where(sent_flag, -1, facelist[None, :])
    cands = jnp.concatenate([halo_ids, owned_ids], 1)
    total = 4 * CAP + F_DEV
    score = jnp.where(cands < 0, 1, 0) * total + jnp.arange(total, dtype=jnp.int32)[None, :]
    order = jnp.argsort(score, axis=1)
    second = jnp.take_along_axis(cands, order[:, :F_DEV], 1)
    full = jnp.concatenate([jnp.broadcast_to(facelist[None, :], (SUBDOMAINS, F_DEV)), second], 1)
    shuffle_keys = jax.random.split(jax.random.fold_in(key, 13), SUBDOMAINS)
    shuffled = jax.vmap(lambda k, row: row[jax.random.permutation(k, 2 * F_DEV)])(shuffle_keys, full)
    return (shuffled.reshape(SUBDOMAINS * E_DEV, 6).astype(jnp.int32), send.astype(jnp.int32))


def draw_elem_faces(key, part):
    return partition(key)[0]


def draw_send_faces(key, part):
    return partition(key)[1]


def draw_residual(key, part):
    key = jax.random.fold_in(key, 21)
    first, second = jax.random.split(key, 2)
    shape = (SOURCES, 2, TRACES)
    owner = (jnp.arange(TRACES, dtype=jnp.int32) // (F_DEV * FACE_DOF)).astype(jnp.float32)
    amplitude = jnp.exp(0.55 * owner / (SUBDOMAINS - 1))
    rough = jnp.exp(jax.random.uniform(second, (1, 1, SUBDOMAINS * F_DEV), jnp.float32, math.log(0.3), math.log(3.0)))
    rough = jnp.repeat(rough, FACE_DOF, axis=2)
    base = jax.random.normal(first, shape, jnp.float32)
    return jnp.clip(base * rough * amplitude, -24.0, 24.0)


def draw_elem_inv(key, part):
    key = jax.random.fold_in(key, 31)
    kone, ktwo, kthree, kfour = jax.random.split(key, 4)
    count = SUBDOMAINS * E_DEV
    shape = (count, ELEM_DOF, ELEM_DOF)
    scale = 0.5 / math.sqrt(ELEM_DOF)
    diagonal = jnp.arange(ELEM_DOF)[:, None] == jnp.arange(ELEM_DOF)[None, :]
    off_re = jnp.clip(jax.random.normal(kone, shape, jnp.float32), -4.0, 4.0) * scale
    off_im = jnp.clip(jax.random.normal(ktwo, shape, jnp.float32), -4.0, 4.0) * scale
    diag_re = jax.random.uniform(kthree, (count, ELEM_DOF, 1), jnp.float32, 0.8, 1.6)
    diag_im = jax.random.uniform(kfour, (count, ELEM_DOF, 1), jnp.float32, 0.2, 0.8)
    real_part = jnp.where(diagonal, diag_re, off_re)
    imag_part = jnp.where(diagonal, diag_im, off_im)
    stacked = jnp.stack([real_part, imag_part], 1)
    return stacked.reshape(SUBDOMAINS, E_DEV * 2 * ELEM_DOF * ELEM_DOF).astype(jnp.bfloat16)


def draw_coarse_inv(key, part):
    key = jax.random.fold_in(key, 41)
    shape = (2, NCT, NCT)
    base = jnp.clip(jax.random.normal(key, shape, jnp.float32), -5.0, 5.0)
    base = base * 0.005
    return ((base + jnp.swapaxes(base, 1, 2)) * 0.7071).astype(jnp.bfloat16)


def block_levels(rng, dims, cuts, smallest, high):
    level, own = 1.0, jax.random.fold_in(rng, 6)
    for dim, parts in cuts:
        heights = jnp.exp(jax.random.uniform(jax.random.fold_in(own, dim), (parts,), jnp.float32, smallest / len(cuts), high / len(cuts)))
        level = level * jnp.repeat(heights, dims[dim] // parts).reshape([-1 if axis == dim else 1 for axis in range(len(dims))])
    return level


def noise(own_key, shape, width, reach, pieces=(), held_as=jnp.bfloat16):
    entries = jax.random.normal(own_key, shape, jnp.float32) * width
    if len(pieces) > 0:
        entries = block_levels(own_key, shape, pieces, -0.22, 0.18) * entries
    return jnp.clip(entries, min=-reach, max=reach).astype(held_as)


def setup_inputs(seed: int = 0, part: int = 0) -> dict:
    arg_keys = jax.random.split(jax.random.key(seed), 7)
    part_splits = jax.random.split(jax.random.fold_in(arg_keys[6], part), 7)
    return {
        "residual": draw_residual(jax.random.fold_in(jax.random.fold_in(arg_keys[6], part), 71), part),
        "elem_inv": draw_elem_inv(jax.random.fold_in(jax.random.fold_in(arg_keys[6], part), 71), part),
        "elem_faces": draw_elem_faces(jax.random.fold_in(jax.random.fold_in(arg_keys[6], part), 71), part),
        "send_faces": draw_send_faces(jax.random.fold_in(jax.random.fold_in(arg_keys[6], part), 71), part),
        "coarse_basis": noise(part_splits[4], (2, NCT, F_DEV * FACE_DOF), 0.05, 0.29882812, ((1, 8),)),
        "coarse_inv": draw_coarse_inv(jax.random.fold_in(jax.random.fold_in(arg_keys[6], part), 71), part),
    }


NEIGHBOUR_OFFSETS = (-2, -1, 1, 2)


def element_solve(ext_d, ops_d, look_d):
    dead = F_DEV + 4 * CAP
    vec = ext_d[:, :, look_d].reshape(SOURCES, 2, E_DEV, ELEM_DOF).astype(jnp.float32)
    ops = ops_d.astype(jnp.float32)
    out_re = jnp.einsum("eij,sej->sei", ops[:, 0], vec[:, 0]) - jnp.einsum("eij,sej->sei", ops[:, 1], vec[:, 1])
    out_im = jnp.einsum("eij,sej->sei", ops[:, 0], vec[:, 1]) + jnp.einsum("eij,sej->sei", ops[:, 1], vec[:, 0])
    local = jnp.stack([out_re, out_im], 1).reshape(SOURCES, 2, E_DEV * 6, FACE_DOF)
    return jax.ops.segment_sum(jnp.moveaxis(local, 2, 0), look_d, num_segments=dead + 1)


def reference(residual, elem_inv, elem_faces, send_faces, coarse_basis, coarse_inv):
    rounded = residual.astype(jnp.bfloat16)
    subs = SUBDOMAINS
    dead = F_DEV + 4 * CAP
    faces = rounded.reshape(SOURCES, 2, subs, F_DEV, FACE_DOF)
    zero_face = jnp.zeros((SOURCES, 2, subs, 1, FACE_DOF), jnp.bfloat16)
    padded = jnp.concatenate([faces, zero_face], 3)
    outgoing = jnp.where(send_faces < 0, F_DEV, send_faces).astype(jnp.int32)
    ident = jnp.arange(subs, dtype=jnp.int32)
    halos = []
    for slot, offset in enumerate(NEIGHBOUR_OFFSETS):
        source = ident + offset
        valid = (source >= 0) & (source < subs)
        clipped = jnp.clip(source, 0, subs - 1)
        index = outgoing[clipped, slot]
        taken = padded[:, :, clipped[:, None], index]
        halos.append(jnp.where(valid[None, None, :, None, None], taken, jnp.zeros_like(taken)))
    extended = jnp.concatenate([faces] + halos + [zero_face], 3)
    lookup = jnp.where(elem_faces < 0, dead, elem_faces).astype(jnp.int32).reshape(subs, E_DEV * 6)
    ops_all = elem_inv.reshape(subs, E_DEV, 2, ELEM_DOF, ELEM_DOF)
    summed = lax.map(lambda item: element_solve(item[0], item[1], item[2]),
                     (jnp.moveaxis(extended, 2, 0), ops_all, lookup))
    returned = jnp.zeros((subs, F_DEV + 1, SOURCES, 2, FACE_DOF), jnp.float32)
    for slot, offset in enumerate(NEIGHBOUR_OFFSETS):
        dest = ident - offset
        valid = (dest >= 0) & (dest < subs)
        clipped = jnp.clip(dest, 0, subs - 1)
        part = summed[clipped, F_DEV + slot * CAP:F_DEV + (slot + 1) * CAP]
        part = jnp.where(valid[:, None, None, None, None], part, jnp.zeros_like(part))
        added = jax.vmap(lambda values, index: jax.ops.segment_sum(values, index, num_segments=F_DEV + 1))(part, outgoing[:, slot])
        returned = returned + added
    fine = summed[:, :F_DEV] + returned[:, :F_DEV]
    fine = jnp.transpose(fine, (2, 3, 0, 1, 4)).reshape(SOURCES, 2, TRACES)
    length = F_DEV * FACE_DOF
    basis = coarse_basis.reshape(2, subs, NCOARSE, length).astype(jnp.float32)
    res = rounded.reshape(SOURCES, 2, subs, length).astype(jnp.float32)
    rest_re = jnp.einsum("dkl,sdl->dks", basis[0], res[:, 0]) - jnp.einsum("dkl,sdl->dks", basis[1], res[:, 1])
    rest_im = jnp.einsum("dkl,sdl->dks", basis[0], res[:, 1]) + jnp.einsum("dkl,sdl->dks", basis[1], res[:, 0])
    rest_re = rest_re.reshape(NCT, SOURCES).astype(jnp.bfloat16)
    rest_im = rest_im.reshape(NCT, SOURCES).astype(jnp.bfloat16)
    coeff_re = jnp.dot(coarse_inv[0], rest_re, preferred_element_type=jnp.float32) - jnp.dot(coarse_inv[1], rest_im, preferred_element_type=jnp.float32)
    coeff_im = jnp.dot(coarse_inv[0], rest_im, preferred_element_type=jnp.float32) + jnp.dot(coarse_inv[1], rest_re, preferred_element_type=jnp.float32)
    cb_re = coeff_re.astype(jnp.bfloat16).astype(jnp.float32).reshape(subs, NCOARSE, SOURCES)
    cb_im = coeff_im.astype(jnp.bfloat16).astype(jnp.float32).reshape(subs, NCOARSE, SOURCES)
    coarse_re = jnp.einsum("dks,dkl->sdl", cb_re, basis[0]) - jnp.einsum("dks,dkl->sdl", cb_im, basis[1])
    coarse_im = jnp.einsum("dks,dkl->sdl", cb_re, basis[1]) + jnp.einsum("dks,dkl->sdl", cb_im, basis[0])
    coarse = jnp.stack([coarse_re.reshape(SOURCES, TRACES), coarse_im.reshape(SOURCES, TRACES)], 1)
    precond = fine + coarse
    rf = rounded.astype(jnp.float32)
    inner_re = jnp.sum(rf[:, 0] * precond[:, 0] + rf[:, 1] * precond[:, 1], -1)
    inner_im = jnp.sum(rf[:, 0] * precond[:, 1] - rf[:, 1] * precond[:, 0], -1)
    inner = jnp.stack([inner_re, inner_im], 1) / TRACES
    return precond, inner
```

```python
import functools

import jax
import jax.numpy as jnp
from jax import lax
from jax.experimental import pallas as pl
from jax.experimental.pallas import tpu as pltpu
from jax.sharding import PartitionSpec as P

FACE_DOF = 25
OFFSETS = (-2, -1, 1, 2)
BF = jnp.bfloat16
F32 = jnp.float32
MESH = pl.DeviceIdType.MESH


def iota(shape, dim):
    return lax.broadcasted_iota(jnp.int32, shape, dim)


def over_25(index):
    return jnp.floor((index.astype(F32) + 0.5) * (1.0 / FACE_DOF)).astype(jnp.int32)


def dot_nt(left, right):
    return lax.dot_general(left, right, (((1,), (1,)), ((), ())), preferred_element_type=F32)


def dot_nn(left, right):
    return lax.dot_general(left, right, (((1,), (0,)), ((), ())), preferred_element_type=F32)


def split2(values):
    high = values.astype(BF)
    return high, (values - high.astype(F32)).astype(BF)


def loop(count, body):
    if count <= 16:
        for i in range(count):
            body(i)
    else:
        def step(i, carry):
            body(i)
            return carry
        lax.fori_loop(0, count, step, 0)


def kernel(
    nsub, ncoarse, total,
    res_ref, elem_ref, faces_ref, send_ref, basis_ref, cinv_ref,
    out_ref, inner_ref,
    flat, rows128, mat0, mat1, v6, ext, xs0, xs1, ys0, ys1,
    halo_out, halo_in, rest_out, rest_in, cfull, ret_out, ret_in, inner_out, inner_in,
    elem_sem, halo_send, halo_recv, rest_send, rest_recv, cinv_send, cinv_recv,
    ret_send, ret_recv, inner_send, inner_recv,
):
    nall = nsub * ncoarse
    length = res_ref.shape[2]
    owned = length // FACE_DOF
    slots = 4 * send_ref.shape[2]
    nelem = faces_ref.shape[1]
    ext_rows = owned + slots
    edof = 6 * FACE_DOF
    nslot = 6 * nelem
    rep = lax.axis_index("rep")
    me = lax.axis_index("sub") * ncoarse + lax.axis_index("coarse")

    elem_copy = pltpu.make_async_copy(elem_ref, flat, elem_sem)
    elem_copy.start()

    def where_is(other):
        return {"sub": other // ncoarse, "coarse": lax.rem(other, ncoarse)}

    def peer(i):
        return lax.rem(me + i + 1, nall)

    barrier = pltpu.get_barrier_semaphore()
    loop(nall - 1, lambda i: pl.semaphore_signal(
        barrier, inc=1, device_id=where_is(peer(i)), device_id_type=MESH))
    pl.semaphore_signal(barrier, inc=1, device_id={"rep": 1 - rep}, device_id_type=MESH)

    rb = jnp.concatenate([res_ref[:, 0, :], res_ref[:, 1, :]], 0).astype(BF)
    rf = rb.astype(F32)
    sign = jnp.where(iota((8, 1), 0) < 4, -1.0, 1.0).astype(F32)

    trace = iota((1, length), 1)
    trace_face = over_25(trace)
    trace_dof = trace - FACE_DOF * trace_face
    face_mask = iota((owned, length), 0) == trace_face
    face_bf = jnp.where(face_mask, 1.0, 0.0).astype(BF)
    lane_col = iota((256, 1), 0)
    lane_dof = jnp.where(lane_col < edof, lane_col - FACE_DOF * over_25(lane_col), -1)
    v6[...] = jnp.where(lane_dof == trace_dof, 1.0, 0.0).astype(BF)

    basis = basis_ref[...].reshape(128, length)
    q = dot_nt(rb, basis)
    rest = q + sign * pltpu.roll(pltpu.roll(q, 64, 1), 4, 0)
    rest = jnp.where(iota((8, 128), 1) < 64, rest.astype(BF).astype(F32), 0.0)
    rest = jnp.where(lax.rem(me, 2) == 1, pltpu.roll(rest, 64, 1), rest)
    rest_out[...] = rest
    rest_in[pl.ds(me, 1)] = rest[None]

    id_row = jnp.concatenate(
        [faces_ref[k:k + 1, :] for k in range(6)] + [send_ref[0, j:j + 1, :] for j in range(4)], 1)
    pick_t = jnp.where(iota((128, 128), 0) == id_row, 1.0, 0.0).astype(F32)
    pick = pick_t.T
    send_id = jnp.sum(pick[nslot:] * (iota((slots, 128), 1) + 1).astype(F32), 1, keepdims=True) - 1.0
    pick_b = pick.astype(BF)
    gather = pick_b[:nslot, :ext_rows]
    packer = pick_b[nslot:, :owned]

    left = jnp.concatenate([face_bf * rb[i:i + 1, :] for i in range(8)], 0)
    tiled = dot_nt(left, v6[...])
    packed = []
    for i in range(8):
        part = tiled[i * owned:(i + 1) * owned]
        ext[i, 0:owned, :] = part
        packed.append(dot_nn(packer, part[:, :128].astype(BF)))
    for j in range(4):
        halo_out[j] = jnp.concatenate([part[j * 8:(j + 1) * 8] for part in packed], 0).astype(BF)

    pl.semaphore_wait(barrier, nall)

    def halo_copy(j):
        return pltpu.make_async_remote_copy(
            src_ref=halo_out.at[j], dst_ref=halo_in.at[j], send_sem=halo_send.at[j],
            recv_sem=halo_recv.at[j], device_id=where_is(jnp.clip(me - OFFSETS[j], 0, nall - 1)),
            device_id_type=MESH)

    def ret_copy(j):
        return pltpu.make_async_remote_copy(
            src_ref=ret_out.at[j], dst_ref=ret_in.at[j], send_sem=ret_send.at[j],
            recv_sem=ret_recv.at[j], device_id=where_is(jnp.clip(me + OFFSETS[j], 0, nall - 1)),
            device_id_type=MESH)

    def rest_copy(i, block):
        return pltpu.make_async_remote_copy(
            src_ref=rest_out, dst_ref=rest_in.at[block], send_sem=rest_send.at[i],
            recv_sem=rest_recv.at[block], device_id=where_is(peer(i)), device_id_type=MESH)

    def inner_copy(i, block):
        return pltpu.make_async_remote_copy(
            src_ref=inner_out, dst_ref=inner_in.at[block], send_sem=inner_send.at[i],
            recv_sem=inner_recv.at[block], device_id=where_is(peer(i)), device_id_type=MESH)

    def cinv_copy(half):
        return pltpu.make_async_remote_copy(
            src_ref=cinv_ref, dst_ref=cfull.at[half], send_sem=cinv_send,
            recv_sem=cinv_recv, device_id={"rep": 1 - rep}, device_id_type=MESH)

    def has_reader(j):
        return (me - OFFSETS[j] >= 0) & (me - OFFSETS[j] < nall)

    def has_source(j):
        return (me + OFFSETS[j] >= 0) & (me + OFFSETS[j] < nall)

    for j in range(4):
        @pl.when(has_reader(j))
        def _():
            halo_copy(j).start()

    loop(nall - 1, lambda i: rest_copy(i, me).start())
    cinv_copy(rep).start()
    cfull[pl.ds(rep, 1)] = cinv_ref[...][None]

    elem_copy.wait()
    per = 75 * 128

    def widen(i, carry):
        start = pl.multiple_of(i * per, 128)
        rows128[pl.ds(i * 75, 75), :] = flat[0:1, pl.ds(start, per)].astype(F32).reshape(75, 128)
        return carry

    lax.fori_loop(0, 75, widen, 0, unroll=5)
    lane75 = iota((75, 128), 1)

    def regroup(i, carry):
        first = (150 * i) // 128
        shift = 128 - (150 * i - 128 * first)
        a = pltpu.roll(rows128[pl.ds(first, 75, stride=75), :], shift, 1)
        b = pltpu.roll(rows128[pl.ds(first + 1, 75, stride=75), :], shift, 1)
        c = pltpu.roll(rows128[pl.ds(first + 2, 75, stride=75), :], shift, 1)
        mat0[pl.ds(i, 75, stride=64), :] = jnp.where(lane75 < shift, a, b)
        mat1[pl.ds(i, 75, stride=64), :] = jnp.where(
            lane75 < edof - 128, jnp.where(lane75 < shift, b, c), 0.0)
        return carry

    lax.fori_loop(0, 64, regroup, 0, unroll=8)

    for j in range(4):
        @pl.when(has_source(j))
        def _():
            halo_copy(j).wait_recv()

        @pl.when(jnp.logical_not(has_source(j)))
        def _():
            halo_in[j] = jnp.zeros((64, 128), BF)

        half0 = halo_in[j].astype(F32)
        half1 = pltpu.roll(half0, 125, 1)
        for i in range(8):
            at = owned + j * 8
            ext[i, at:at + 8, 0:128] = half0[i * 8:(i + 1) * 8]
            ext[i, at:at + 8, 128:256] = half1[i * 8:(i + 1) * 8]

    lane_face = over_25(iota((1, 256), 1))
    slot_col = jnp.concatenate([jnp.full((nelem, 1), k, jnp.int32) for k in range(6)], 0)
    slot_mask = lane_face == slot_col
    for i in range(8):
        taken = jnp.where(slot_mask, dot_nn(gather, ext[i].astype(BF)), 0.0)
        x = taken[:nelem]
        for k in range(1, 6):
            x = x + taken[k * nelem:(k + 1) * nelem]
        xs0[i * nelem:(i + 1) * nelem, :] = x[:, :128]
        xs1[i * nelem:(i + 1) * nelem, :] = x[:, 128:]

    fill = jnp.zeros((8, 256 - edof), F32)
    for e in range(nelem):
        xa = jnp.concatenate(
            [xs0[pl.ds(e, 8, stride=nelem), :], xs1[pl.ds(e, 8, stride=nelem), :]], 1)
        xb = sign * pltpu.roll(xa, 4, 0)
        at = e * 2 * edof
        op_re = jnp.concatenate([mat0[at:at + edof, :], mat1[at:at + edof, :]], 1).astype(BF)
        at = at + edof
        op_im = jnp.concatenate([mat0[at:at + edof, :], mat1[at:at + edof, :]], 1).astype(BF)
        y = dot_nt(xa.astype(BF), op_re) + dot_nt(xb.astype(BF), op_im)
        y = jnp.concatenate([y, fill], 1)
        ys0[pl.ds(e, 8, stride=nelem), :] = y[:, :128]
        ys1[pl.ds(e, 8, stride=nelem), :] = y[:, 128:]

    scatter = pick_t.astype(BF)[:ext_rows, :nslot]
    scatter = jnp.concatenate([scatter, scatter], 1)
    summed = []
    for i in range(8):
        rows = slice(i * nelem, (i + 1) * nelem)
        y = jnp.concatenate([ys0[rows, :], ys1[rows, :]], 1)
        y = jnp.where(slot_mask, jnp.concatenate([y] * 6, 0), 0.0)
        high, low = split2(y)
        summed.append(dot_nn(scatter, jnp.concatenate([high, low], 0)))
    fold_lane = iota((1, 128), 1)
    fold = jnp.where((lane_dof == fold_lane), 1.0, 0.0).astype(BF)
    back = jnp.concatenate(
        [s[owned + j * 8:owned + (j + 1) * 8] for j in range(4) for s in summed], 0)
    high, low = split2(back)
    back = dot_nn(high, fold) + dot_nn(low, fold)
    for j in range(4):
        ret_out[j] = back[j * 64:(j + 1) * 64]

        @pl.when(has_source(j))
        def _():
            ret_copy(j).start()

    def rest_wait(i):
        rest_copy(i, peer(i)).wait_recv()

    loop(nall - 1, rest_wait)
    cinv_copy(1 - rep).wait_recv()
    rest_all = jnp.concatenate(
        [rest_in[2 * p] + rest_in[2 * p + 1] for p in range(nall // 2)], 1).astype(BF)
    w = dot_nt(rest_all, cfull[...].reshape(128, rest_all.shape[1]))
    w = w + sign * pltpu.roll(pltpu.roll(w, 96, 1), 4, 0)
    lane128 = iota((8, 128), 1)
    co = jnp.where(lane128 < 32, w, pltpu.roll(w, 96, 1))[:, :64].astype(BF)
    basis = basis_ref[...]
    coarse = dot_nn(co, basis[0]) + sign * pltpu.roll(dot_nn(co, basis[1]), 4, 0)

    half = 4 * nelem
    x0, x1, y0, y1 = xs0[...], xs1[...], ys0[...], ys1[...]
    part_re = x0 * y0 + x1 * y1
    part_im = x0 * pltpu.roll(y0, half, 0) + x1 * pltpu.roll(y1, half, 0)
    part_re = jnp.sum(part_re.reshape(8, nelem, 128), 1)
    part_im = jnp.sum(part_im.reshape(8, nelem, 128), 1)
    part_re = jnp.sum(part_re, 1, keepdims=True) + jnp.sum(rf * coarse, 1, keepdims=True)
    part_im = jnp.sum(part_im, 1, keepdims=True) + jnp.sum(
        rf * pltpu.roll(coarse, 4, 0), 1, keepdims=True)
    part_im = -sign * part_im
    part_re = jnp.broadcast_to(part_re, (8, 128))
    part_im = jnp.broadcast_to(part_im, (8, 128))
    part_re = part_re + pltpu.roll(part_re, 4, 0)
    part_im = part_im + pltpu.roll(part_im, 4, 0)
    mine = jnp.where(lane128 == 0, part_re, part_im)
    inner_out[...] = mine
    inner_in[pl.ds(me, 1)] = mine[None]
    loop(nall - 1, lambda i: inner_copy(i, me).start())

    result = []
    for i in range(8):
        high, low = split2(summed[i][:owned])
        wide = dot_nn(high, v6[...]) + dot_nn(low, v6[...])
        result.append(jnp.sum(jnp.where(face_mask, wide, 0.0), 0, keepdims=True))
    result = jnp.concatenate(result, 0) + coarse

    for j in range(4):
        @pl.when(has_reader(j))
        def _():
            ret_copy(j).wait_recv()

        @pl.when(jnp.logical_not(has_reader(j)))
        def _():
            ret_in[j] = jnp.zeros((64, 128), F32)

    send_mask = send_id.astype(jnp.int32) == trace_face
    given = []
    for i in range(8):
        got = jnp.concatenate([ret_in[j, i * 8:(i + 1) * 8, :] for j in range(4)], 0)
        high = got.astype(BF).astype(F32)
        got = (high + pltpu.roll(got - high, FACE_DOF, 1)).astype(BF)
        wide = dot_nn(got, v6[0:128, :])
        given.append(jnp.sum(jnp.where(send_mask, wide, 0.0), 0, keepdims=True))
    result = result + jnp.concatenate(given, 0)
    out_ref[:, 0, :] = result[0:4]
    out_ref[:, 1, :] = result[4:8]

    loop(nall - 1, lambda i: inner_copy(i, peer(i)).wait_recv())
    inner_ref[...] = jnp.sum(inner_in[...], 0)[0:4, 0:2] * (1.0 / total)

    for j in range(4):
        @pl.when(has_reader(j))
        def _():
            halo_copy(j).wait_send()

        @pl.when(has_source(j))
        def _():
            ret_copy(j).wait_send()

    cinv_copy(rep).wait_send()

    def sent(i):
        rest_copy(i, me).wait_send()
        inner_copy(i, me).wait_send()

    loop(nall - 1, sent)


def solution(mesh):
    nsub = mesh.shape["sub"]
    ncoarse = mesh.shape["coarse"]
    nall = nsub * ncoarse
    placed = (
        P("rep", None, ("groups", "sub", "coarse")),
        P(("groups", "sub", "coarse"), None),
        P(("groups", "sub", "coarse"), None),
        P(("groups", "sub", "coarse"), None, None),
        P(None, ("groups", "sub", "coarse"), None),
        P(None, ("groups", "sub", "coarse", "rep"), None),
    )

    def on_device(residual, elem_inv, elem_faces, send_faces, coarse_basis, coarse_inv):
        length = residual.shape[2]
        count = elem_inv.shape[1]
        vmem = pl.BlockSpec(memory_space=pltpu.VMEM)
        anywhere = pl.BlockSpec(memory_space=pl.ANY)
        dma = pltpu.SemaphoreType.DMA
        return pl.pallas_call(
            functools.partial(kernel, nsub, ncoarse, length * nall),
            out_shape=(
                jax.ShapeDtypeStruct(residual.shape, F32),
                jax.ShapeDtypeStruct((residual.shape[0], 2), F32),
            ),
            in_specs=[vmem, anywhere, vmem, vmem, vmem, vmem],
            out_specs=(vmem, vmem),
            scratch_shapes=[
                pltpu.VMEM((1, count), BF),
                pltpu.VMEM((count // 128 + 7, 128), F32),
                pltpu.VMEM((count // 150, 128), F32),
                pltpu.VMEM((count // 150, 128), F32),
                pltpu.VMEM((256, length), BF),
                pltpu.VMEM((8, 80, 256), F32),
                pltpu.VMEM((128, 128), F32),
                pltpu.VMEM((128, 128), F32),
                pltpu.VMEM((128, 128), F32),
                pltpu.VMEM((128, 128), F32),
                pltpu.VMEM((4, 64, 128), BF),
                pltpu.VMEM((4, 64, 128), BF),
                pltpu.VMEM((8, 128), F32),
                pltpu.VMEM((nall, 8, 128), F32),
                pltpu.VMEM((2,) + coarse_inv.shape, BF),
                pltpu.VMEM((4, 64, 128), F32),
                pltpu.VMEM((4, 64, 128), F32),
                pltpu.VMEM((8, 128), F32),
                pltpu.VMEM((nall, 8, 128), F32),
                dma, dma((4,)), dma((4,)), dma((nall,)), dma((nall,)), dma, dma,
                dma((4,)), dma((4,)), dma((nall,)), dma((nall,)),
            ],
            compiler_params=pltpu.CompilerParams(
                collective_id=0, has_side_effects=True, vmem_limit_bytes=56 << 20),
        )(residual, elem_inv, elem_faces.T, send_faces, coarse_basis, coarse_inv)

    return jax.shard_map(
        on_device,
        mesh=mesh,
        in_specs=placed,
        out_specs=(P("rep", None, ("groups", "sub", "coarse")), P(("groups", "rep"), None)),
        check_vma=False,
    )
```

```python
import functools

import jax
import jax.numpy as jnp
from jax import lax
from jax.experimental import pallas as pl
from jax.experimental.pallas import tpu as pltpu
from jax.sharding import PartitionSpec as P

FACE_DOF = 25
OFFSETS = (-2, -1, 1, 2)
BF = jnp.bfloat16
F32 = jnp.float32
MESH = pl.DeviceIdType.MESH


def iota(shape, dim):
    return lax.broadcasted_iota(jnp.int32, shape, dim)


def over_25(index):
    return jnp.floor((index.astype(F32) + 0.5) * (1.0 / FACE_DOF)).astype(jnp.int32)


def dot_nt(left, right):
    return lax.dot_general(left, right, (((1,), (1,)), ((), ())), preferred_element_type=F32)


def dot_nn(left, right):
    return lax.dot_general(left, right, (((1,), (0,)), ((), ())), preferred_element_type=F32)


def split2(values):
    high = values.astype(BF)
    return high, (values - high.astype(F32)).astype(BF)


def loop(count, body):
    if count <= 16:
        for i in range(count):
            body(i)
    else:
        def step(i, carry):
            body(i)
            return carry
        lax.fori_loop(0, count, step, 0)


def kernel(
    nsub, ncoarse, total,
    res_ref, elem_ref, faces_ref, send_ref, basis_ref, cinv_ref,
    out_ref,
    flat, rows128, mat0, mat1, v6, ext, xs0, xs1, ys0, ys1,
    halo_out, halo_in, rest_out, rest_in, cfull, ret_out, ret_in, inner_out, inner_in,
    elem_sem, halo_send, halo_recv, rest_send, rest_recv, cinv_send, cinv_recv,
    ret_send, ret_recv, inner_send, inner_recv,
):
    nall = nsub * ncoarse
    length = res_ref.shape[2]
    owned = length // FACE_DOF
    slots = 4 * send_ref.shape[2]
    nelem = faces_ref.shape[1]
    ext_rows = owned + slots
    edof = 6 * FACE_DOF
    nslot = 6 * nelem
    rep = lax.axis_index("rep")
    me = lax.axis_index("sub") * ncoarse + lax.axis_index("coarse")

    elem_copy = pltpu.make_async_copy(elem_ref, flat, elem_sem)
    elem_copy.start()

    def where_is(other):
        return {"sub": other // ncoarse, "coarse": lax.rem(other, ncoarse)}

    def peer(i):
        return lax.rem(me + i + 1, nall)

    barrier = pltpu.get_barrier_semaphore()
    loop(nall - 1, lambda i: pl.semaphore_signal(
        barrier, inc=1, device_id=where_is(peer(i)), device_id_type=MESH))
    pl.semaphore_signal(barrier, inc=1, device_id={"rep": 1 - rep}, device_id_type=MESH)

    rb = jnp.concatenate([res_ref[:, 0, :], res_ref[:, 1, :]], 0).astype(BF)
    rf = rb.astype(F32)
    sign = jnp.where(iota((8, 1), 0) < 4, -1.0, 1.0).astype(F32)

    trace = iota((1, length), 1)
    trace_face = over_25(trace)
    trace_dof = trace - FACE_DOF * trace_face
    face_mask = iota((owned, length), 0) == trace_face
    face_bf = jnp.where(face_mask, 1.0, 0.0).astype(BF)
    lane_col = iota((256, 1), 0)
    lane_dof = jnp.where(lane_col < edof, lane_col - FACE_DOF * over_25(lane_col), -1)
    v6[...] = jnp.where(lane_dof == trace_dof, 1.0, 0.0).astype(BF)

    basis = basis_ref[...].reshape(128, length)
    q = dot_nt(rb, basis)
    rest = q + sign * pltpu.roll(pltpu.roll(q, 64, 1), 4, 0)
    rest = jnp.where(iota((8, 128), 1) < 64, rest.astype(BF).astype(F32), 0.0)
    rest = jnp.where(lax.rem(me, 2) == 1, pltpu.roll(rest, 64, 1), rest)
    rest_out[...] = rest
    rest_in[pl.ds(me, 1)] = rest[None]

    id_row = jnp.concatenate(
        [faces_ref[k:k + 1, :] for k in range(6)] + [send_ref[0, j:j + 1, :] for j in range(4)], 1)
    pick_t = jnp.where(iota((128, 128), 0) == id_row, 1.0, 0.0).astype(F32)
    pick = pick_t.T
    send_id = jnp.sum(pick[nslot:] * (iota((slots, 128), 1) + 1).astype(F32), 1, keepdims=True) - 1.0
    pick_b = pick.astype(BF)
    gather = pick_b[:nslot, :ext_rows]
    packer = pick_b[nslot:, :owned]

    left = jnp.concatenate([face_bf * rb[i:i + 1, :] for i in range(8)], 0)
    tiled = dot_nt(left, v6[...])
    packed = []
    for i in range(8):
        part = tiled[i * owned:(i + 1) * owned]
        ext[i, 0:owned, :] = part
        packed.append(dot_nn(packer, part[:, :128].astype(BF)))
    for j in range(4):
        halo_out[j] = jnp.concatenate([part[j * 8:(j + 1) * 8] for part in packed], 0).astype(BF)

    pl.semaphore_wait(barrier, nall)

    def halo_copy(j):
        return pltpu.make_async_remote_copy(
            src_ref=halo_out.at[j], dst_ref=halo_in.at[j], send_sem=halo_send.at[j],
            recv_sem=halo_recv.at[j], device_id=where_is(jnp.clip(me - OFFSETS[j], 0, nall - 1)),
            device_id_type=MESH)

    def ret_copy(j):
        return pltpu.make_async_remote_copy(
            src_ref=ret_out.at[j], dst_ref=ret_in.at[j], send_sem=ret_send.at[j],
            recv_sem=ret_recv.at[j], device_id=where_is(jnp.clip(me + OFFSETS[j], 0, nall - 1)),
            device_id_type=MESH)

    def rest_copy(i, block):
        return pltpu.make_async_remote_copy(
            src_ref=rest_out, dst_ref=rest_in.at[block], send_sem=rest_send.at[i],
            recv_sem=rest_recv.at[block], device_id=where_is(peer(i)), device_id_type=MESH)

    def inner_copy(i, block):
        return pltpu.make_async_remote_copy(
            src_ref=inner_out, dst_ref=inner_in.at[block], send_sem=inner_send.at[i],
            recv_sem=inner_recv.at[block], device_id=where_is(peer(i)), device_id_type=MESH)

    def cinv_copy(half):
        return pltpu.make_async_remote_copy(
            src_ref=cinv_ref, dst_ref=cfull.at[half], send_sem=cinv_send,
            recv_sem=cinv_recv, device_id={"rep": 1 - rep}, device_id_type=MESH)

    def has_reader(j):
        return (me - OFFSETS[j] >= 0) & (me - OFFSETS[j] < nall)

    def has_source(j):
        return (me + OFFSETS[j] >= 0) & (me + OFFSETS[j] < nall)

    for j in range(4):
        @pl.when(has_reader(j))
        def _():
            halo_copy(j).start()

    loop(nall - 1, lambda i: rest_copy(i, me).start())
    cinv_copy(rep).start()
    cfull[pl.ds(rep, 1)] = cinv_ref[...][None]

    elem_copy.wait()
    count = flat.shape[1]
    nrows = count // 128
    full = nrows // 64

    def widen(i, carry):
        start = pl.multiple_of(i * 8192, 8192)
        to = pl.multiple_of(i * 64, 64)
        rows128[pl.ds(to, 64), :] = flat[0:1, pl.ds(start, 8192)].astype(F32).reshape(64, 128)
        return carry

    lax.fori_loop(0, full, widen, 0, unroll=3)
    rest_rows = nrows - full * 64
    rows128[full * 64:nrows, :] = flat[0:1, full * 8192:count].astype(F32).reshape(rest_rows, 128)
    lane75 = iota((75, 128), 1)
    for i in range(64):
        first = (edof * i) // 128
        skip = edof * i - 128 * first
        shift = 128 - skip

        def turned(row):
            block = rows128[pl.ds(row, 75, stride=75), :]
            return pltpu.roll(block, shift, 1) if skip else block

        a = turned(first)
        b = turned(first + 1)
        mat0[pl.ds(i, 75, stride=64), :] = jnp.where(lane75 < shift, a, b) if skip else a
        mat1[pl.ds(i, 75, stride=64), :] = (
            jnp.where(lane75 < shift, b, turned(first + 2)) if skip + edof > 256 else b)

    for j in range(4):
        @pl.when(has_source(j))
        def _():
            halo_copy(j).wait_recv()

        @pl.when(jnp.logical_not(has_source(j)))
        def _():
            halo_in[j] = jnp.zeros((64, 128), BF)

        half0 = halo_in[j].astype(F32)
        half1 = pltpu.roll(half0, 125, 1)
        for i in range(8):
            at = owned + j * 8
            ext[i, at:at + 8, 0:128] = half0[i * 8:(i + 1) * 8]
            ext[i, at:at + 8, 128:256] = half1[i * 8:(i + 1) * 8]

    lane_face = over_25(iota((1, 256), 1))
    slot_col = jnp.concatenate([jnp.full((nelem, 1), k, jnp.int32) for k in range(6)], 0)
    slot_mask = lane_face == slot_col
    for i in range(8):
        taken = jnp.where(slot_mask, dot_nn(gather, ext[i].astype(BF)), 0.0)
        x = taken[:nelem]
        for k in range(1, 6):
            x = x + taken[k * nelem:(k + 1) * nelem]
        xs0[i * nelem:(i + 1) * nelem, :] = x[:, :128]
        xs1[i * nelem:(i + 1) * nelem, :] = x[:, 128:]

    fill = jnp.zeros((8, 256 - edof), F32)
    for e in range(nelem):
        xa = jnp.concatenate(
            [xs0[pl.ds(e, 8, stride=nelem), :], xs1[pl.ds(e, 8, stride=nelem), :]], 1)
        xb = sign * pltpu.roll(xa, 4, 0)
        at = e * 2 * edof
        op_re = jnp.concatenate([mat0[at:at + edof, :], mat1[at:at + edof, :]], 1).astype(BF)
        at = at + edof
        op_im = jnp.concatenate([mat0[at:at + edof, :], mat1[at:at + edof, :]], 1).astype(BF)
        y = dot_nt(xa.astype(BF), op_re) + dot_nt(xb.astype(BF), op_im)
        y = jnp.concatenate([y, fill], 1)
        ys0[pl.ds(e, 8, stride=nelem), :] = y[:, :128]
        ys1[pl.ds(e, 8, stride=nelem), :] = y[:, 128:]

    scatter = pick_t.astype(BF)[:ext_rows, :nslot]
    scatter = jnp.concatenate([scatter, scatter], 1)
    summed = []
    for i in range(8):
        rows = slice(i * nelem, (i + 1) * nelem)
        y = jnp.concatenate([ys0[rows, :], ys1[rows, :]], 1)
        y = jnp.where(slot_mask, jnp.concatenate([y] * 6, 0), 0.0)
        high, low = split2(y)
        summed.append(dot_nn(scatter, jnp.concatenate([high, low], 0)))
    fold_lane = iota((1, 128), 1)
    fold = jnp.where((lane_dof == fold_lane), 1.0, 0.0).astype(BF)
    back = jnp.concatenate(
        [s[owned + j * 8:owned + (j + 1) * 8] for j in range(4) for s in summed], 0)
    high, low = split2(back)
    back = dot_nn(high, fold) + dot_nn(low, fold)
    for j in range(4):
        ret_out[j] = back[j * 64:(j + 1) * 64]

        @pl.when(has_source(j))
        def _():
            ret_copy(j).start()

    def rest_wait(i):
        rest_copy(i, peer(i)).wait_recv()

    loop(nall - 1, rest_wait)
    cinv_copy(1 - rep).wait_recv()
    rest_all = jnp.concatenate(
        [rest_in[2 * p] + rest_in[2 * p + 1] for p in range(nall // 2)], 1).astype(BF)
    w = dot_nt(rest_all, cfull[...].reshape(128, rest_all.shape[1]))
    w = w + sign * pltpu.roll(pltpu.roll(w, 96, 1), 4, 0)
    lane128 = iota((8, 128), 1)
    co = jnp.where(lane128 < 32, w, pltpu.roll(w, 96, 1))[:, :64].astype(BF)
    basis = basis_ref[...]
    coarse = dot_nn(co, basis[0]) + sign * pltpu.roll(dot_nn(co, basis[1]), 4, 0)

    half = 4 * nelem
    x0, x1, y0, y1 = xs0[...], xs1[...], ys0[...], ys1[...]
    part_re = x0 * y0 + x1 * y1
    part_im = x0 * pltpu.roll(y0, half, 0) + x1 * pltpu.roll(y1, half, 0)
    part_re = jnp.sum(part_re.reshape(8, nelem, 128), 1)
    part_im = jnp.sum(part_im.reshape(8, nelem, 128), 1)
    part_re = jnp.sum(part_re, 1, keepdims=True) + jnp.sum(rf * coarse, 1, keepdims=True)
    part_im = jnp.sum(part_im, 1, keepdims=True) + jnp.sum(
        rf * pltpu.roll(coarse, 4, 0), 1, keepdims=True)
    part_im = -sign * part_im
    part_re = jnp.broadcast_to(part_re, (8, 128))
    part_im = jnp.broadcast_to(part_im, (8, 128))
    part_re = part_re + pltpu.roll(part_re, 4, 0)
    part_im = part_im + pltpu.roll(part_im, 4, 0)
    mine = jnp.where(lane128 == 0, part_re, part_im)
    inner_out[...] = mine
    inner_in[pl.ds(me, 1)] = mine[None]
    loop(nall - 1, lambda i: inner_copy(i, me).start())

    result = []
    for i in range(8):
        high, low = split2(summed[i][:owned])
        wide = dot_nn(high, v6[...]) + dot_nn(low, v6[...])
        result.append(jnp.sum(jnp.where(face_mask, wide, 0.0), 0, keepdims=True))
    result = jnp.concatenate(result, 0) + coarse

    for j in range(4):
        @pl.when(has_reader(j))
        def _():
            ret_copy(j).wait_recv()

        @pl.when(jnp.logical_not(has_reader(j)))
        def _():
            ret_in[j] = jnp.zeros((64, 128), F32)

    send_mask = send_id.astype(jnp.int32) == trace_face
    given = []
    for i in range(8):
        got = jnp.concatenate([ret_in[j, i * 8:(i + 1) * 8, :] for j in range(4)], 0)
        high = got.astype(BF).astype(F32)
        got = (high + pltpu.roll(got - high, FACE_DOF, 1)).astype(BF)
        wide = dot_nn(got, v6[0:128, :])
        given.append(jnp.sum(jnp.where(send_mask, wide, 0.0), 0, keepdims=True))
    result = result + jnp.concatenate(given, 0)
    out_ref[:, 0:length] = result
    loop(nall - 1, lambda i: inner_copy(i, peer(i)).wait_recv())
    out_ref[:, length:length + 128] = jnp.sum(inner_in[...], 0) * (1.0 / total)

    for j in range(4):
        @pl.when(has_reader(j))
        def _():
            halo_copy(j).wait_send()

        @pl.when(has_source(j))
        def _():
            ret_copy(j).wait_send()

    cinv_copy(rep).wait_send()

    def sent(i):
        rest_copy(i, me).wait_send()
        inner_copy(i, me).wait_send()

    loop(nall - 1, sent)


def deliver(full_ref, out_ref, inner_ref):
    length = out_ref.shape[2]
    out_ref[:, 0, :] = full_ref[0:4, 0:length]
    out_ref[:, 1, :] = full_ref[4:8, 0:length]
    inner_ref[...] = full_ref[0:4, length:length + 128].T[0:2]


def solution(mesh):
    nsub = mesh.shape["sub"]
    ncoarse = mesh.shape["coarse"]
    nall = nsub * ncoarse
    placed = (
        P("rep", None, ("groups", "sub", "coarse")),
        P(("groups", "sub", "coarse"), None),
        P(("groups", "sub", "coarse"), None),
        P(("groups", "sub", "coarse"), None, None),
        P(None, ("groups", "sub", "coarse"), None),
        P(None, ("groups", "sub", "coarse", "rep"), None),
    )

    def on_device(residual, elem_inv, elem_faces, send_faces, coarse_basis, coarse_inv):
        length = residual.shape[2]
        count = elem_inv.shape[1]
        vmem = pl.BlockSpec(memory_space=pltpu.VMEM)
        anywhere = pl.BlockSpec(memory_space=pl.ANY)
        dma = pltpu.SemaphoreType.DMA
        full = pl.pallas_call(
            functools.partial(kernel, nsub, ncoarse, length * nall),
            out_shape=jax.ShapeDtypeStruct((8, length + 128), F32),
            in_specs=[vmem, anywhere, vmem, vmem, vmem, vmem],
            out_specs=vmem,
            scratch_shapes=[
                pltpu.VMEM((1, count), BF),
                pltpu.VMEM((count // 128 + 7, 128), F32),
                pltpu.VMEM((count // 150, 128), F32),
                pltpu.VMEM((count // 150, 128), F32),
                pltpu.VMEM((256, length), BF),
                pltpu.VMEM((8, 80, 256), F32),
                pltpu.VMEM((128, 128), F32),
                pltpu.VMEM((128, 128), F32),
                pltpu.VMEM((128, 128), F32),
                pltpu.VMEM((128, 128), F32),
                pltpu.VMEM((4, 64, 128), BF),
                pltpu.VMEM((4, 64, 128), BF),
                pltpu.VMEM((8, 128), F32),
                pltpu.VMEM((nall, 8, 128), F32),
                pltpu.VMEM((2,) + coarse_inv.shape, BF),
                pltpu.VMEM((4, 64, 128), F32),
                pltpu.VMEM((4, 64, 128), F32),
                pltpu.VMEM((8, 128), F32),
                pltpu.VMEM((nall, 8, 128), F32),
                dma, dma((4,)), dma((4,)), dma((nall,)), dma((nall,)), dma, dma,
                dma((4,)), dma((4,)), dma((nall,)), dma((nall,)),
            ],
            compiler_params=pltpu.CompilerParams(
                collective_id=0, has_side_effects=True, vmem_limit_bytes=56 << 20),
        )(residual, elem_inv, elem_faces.T, send_faces, coarse_basis, coarse_inv)
        out, inner = pl.pallas_call(
            deliver,
            out_shape=(
                jax.ShapeDtypeStruct(residual.shape, F32),
                jax.ShapeDtypeStruct((2, residual.shape[0]), F32),
            ),
            in_specs=[vmem],
            out_specs=(vmem, vmem),
        )(full)
        return out, inner.T

    return jax.shard_map(
        on_device,
        mesh=mesh,
        in_specs=placed,
        out_specs=(P("rep", None, ("groups", "sub", "coarse")), P(("groups", "rep"), None)),
        check_vma=False,
    )
```

```python
import functools

import jax
import jax.numpy as jnp
from jax import lax
from jax.experimental import pallas as pl
from jax.experimental.pallas import tpu as pltpu
from jax.sharding import PartitionSpec as P

FACE_DOF = 25
OFFSETS = (-2, -1, 1, 2)
BF = jnp.bfloat16
F32 = jnp.float32
MESH = pl.DeviceIdType.MESH


def iota(shape, dim):
    return lax.broadcasted_iota(jnp.int32, shape, dim)


def over_25(index):
    return jnp.floor((index.astype(F32) + 0.5) * (1.0 / FACE_DOF)).astype(jnp.int32)


def dot_nt(left, right):
    return lax.dot_general(left, right, (((1,), (1,)), ((), ())), preferred_element_type=F32)


def dot_nn(left, right):
    return lax.dot_general(left, right, (((1,), (0,)), ((), ())), preferred_element_type=F32)


def split2(values):
    high = values.astype(BF)
    return high, (values - high.astype(F32)).astype(BF)


def loop(count, body):
    if count <= 16:
        for i in range(count):
            body(i)
    else:
        def step(i, carry):
            body(i)
            return carry
        lax.fori_loop(0, count, step, 0)


def kernel(
    nsub, ncoarse, total,
    res_ref, elem_ref, faces_ref, send_ref, basis_ref, cinv_ref,
    out_ref,
    flat, rows128, mat0, mat1, ops, v6, ext, xs0, xs1, ys0, ys1,
    halo_out, halo_in, rest_out, rest_in, cfull, ret_out, ret_in, inner_out, inner_in,
    elem_sem, halo_send, halo_recv, rest_send, rest_recv, cinv_send, cinv_recv,
    ret_send, ret_recv, inner_send, inner_recv,
):
    nall = nsub * ncoarse
    length = res_ref.shape[2]
    owned = length // FACE_DOF
    slots = 4 * send_ref.shape[2]
    nelem = faces_ref.shape[1]
    ext_rows = owned + slots
    edof = 6 * FACE_DOF
    nslot = 6 * nelem
    rep = lax.axis_index("rep")
    me = lax.axis_index("sub") * ncoarse + lax.axis_index("coarse")

    elem_copy = pltpu.make_async_copy(elem_ref, flat, elem_sem)
    elem_copy.start()

    def where_is(other):
        return {"sub": other // ncoarse, "coarse": lax.rem(other, ncoarse)}

    def peer(i):
        return lax.rem(me + i + 1, nall)

    barrier = pltpu.get_barrier_semaphore()
    loop(nall - 1, lambda i: pl.semaphore_signal(
        barrier, inc=1, device_id=where_is(peer(i)), device_id_type=MESH))
    pl.semaphore_signal(barrier, inc=1, device_id={"rep": 1 - rep}, device_id_type=MESH)

    rb = jnp.concatenate([res_ref[:, 0, :], res_ref[:, 1, :]], 0).astype(BF)
    rf = rb.astype(F32)
    sign = jnp.where(iota((8, 1), 0) < 4, -1.0, 1.0).astype(F32)

    trace = iota((1, length), 1)
    trace_face = over_25(trace)
    trace_dof = trace - FACE_DOF * trace_face
    face_mask = iota((owned, length), 0) == trace_face
    face_bf = jnp.where(face_mask, 1.0, 0.0).astype(BF)
    lane_col = iota((256, 1), 0)
    lane_dof = jnp.where(lane_col < edof, lane_col - FACE_DOF * over_25(lane_col), -1)
    v6[...] = jnp.where(lane_dof == trace_dof, 1.0, 0.0).astype(BF)

    basis = basis_ref[...].reshape(128, length)
    q = dot_nt(rb, basis)
    rest = q + sign * pltpu.roll(pltpu.roll(q, 64, 1), 4, 0)
    rest = jnp.where(iota((8, 128), 1) < 64, rest.astype(BF).astype(F32), 0.0)
    rest = jnp.where(lax.rem(me, 2) == 1, pltpu.roll(rest, 64, 1), rest)
    rest_out[...] = rest
    rest_in[pl.ds(me, 1)] = rest[None]

    id_row = jnp.concatenate(
        [faces_ref[k:k + 1, :] for k in range(6)] + [send_ref[0, j:j + 1, :] for j in range(4)], 1)
    pick_t = jnp.where(iota((128, 128), 0) == id_row, 1.0, 0.0).astype(F32)
    pick = pick_t.T
    send_id = jnp.sum(pick[nslot:] * (iota((slots, 128), 1) + 1).astype(F32), 1, keepdims=True) - 1.0
    pick_b = pick.astype(BF)
    gather = pick_b[:nslot, :ext_rows]
    packer = pick_b[nslot:, :owned]

    left = jnp.concatenate([face_bf * rb[i:i + 1, :] for i in range(8)], 0)
    tiled = dot_nt(left, v6[...])
    packed = []
    for i in range(8):
        part = tiled[i * owned:(i + 1) * owned]
        ext[i, 0:owned, :] = part
        packed.append(dot_nn(packer, part[:, :128].astype(BF)))
    for j in range(4):
        halo_out[j] = jnp.concatenate([part[j * 8:(j + 1) * 8] for part in packed], 0).astype(BF)

    pl.semaphore_wait(barrier, nall)

    def halo_copy(j):
        return pltpu.make_async_remote_copy(
            src_ref=halo_out.at[j], dst_ref=halo_in.at[j], send_sem=halo_send.at[j],
            recv_sem=halo_recv.at[j], device_id=where_is(jnp.clip(me - OFFSETS[j], 0, nall - 1)),
            device_id_type=MESH)

    def ret_copy(j):
        return pltpu.make_async_remote_copy(
            src_ref=ret_out.at[j], dst_ref=ret_in.at[j], send_sem=ret_send.at[j],
            recv_sem=ret_recv.at[j], device_id=where_is(jnp.clip(me + OFFSETS[j], 0, nall - 1)),
            device_id_type=MESH)

    def rest_copy(i, block):
        return pltpu.make_async_remote_copy(
            src_ref=rest_out, dst_ref=rest_in.at[block], send_sem=rest_send.at[i],
            recv_sem=rest_recv.at[block], device_id=where_is(peer(i)), device_id_type=MESH)

    def inner_copy(i, block):
        return pltpu.make_async_remote_copy(
            src_ref=inner_out, dst_ref=inner_in.at[block], send_sem=inner_send.at[i],
            recv_sem=inner_recv.at[block], device_id=where_is(peer(i)), device_id_type=MESH)

    def cinv_copy(half):
        return pltpu.make_async_remote_copy(
            src_ref=cinv_ref, dst_ref=cfull.at[half], send_sem=cinv_send,
            recv_sem=cinv_recv, device_id={"rep": 1 - rep}, device_id_type=MESH)

    def has_reader(j):
        return (me - OFFSETS[j] >= 0) & (me - OFFSETS[j] < nall)

    def has_source(j):
        return (me + OFFSETS[j] >= 0) & (me + OFFSETS[j] < nall)

    for j in range(4):
        @pl.when(has_reader(j))
        def _():
            halo_copy(j).start()

    loop(nall - 1, lambda i: rest_copy(i, me).start())
    cinv_copy(rep).start()
    cfull[pl.ds(rep, 1)] = cinv_ref[...][None]

    elem_copy.wait()
    count = flat.shape[1]
    nrows = count // 128
    full = nrows // 64

    def widen(i, carry):
        start = pl.multiple_of(i * 8192, 8192)
        to = pl.multiple_of(i * 64, 64)
        rows128[pl.ds(to, 64), :] = flat[0:1, pl.ds(start, 8192)].astype(F32).reshape(64, 128)
        return carry

    lax.fori_loop(0, full, widen, 0, unroll=3)
    rest_rows = nrows - full * 64
    rows128[full * 64:nrows, :] = flat[0:1, full * 8192:count].astype(F32).reshape(rest_rows, 128)
    lane75 = iota((75, 128), 1)
    for i in range(64):
        first = (edof * i) // 128
        skip = edof * i - 128 * first
        shift = 128 - skip

        def turned(row):
            block = rows128[pl.ds(row, 75, stride=75), :]
            return pltpu.roll(block, shift, 1) if skip else block

        a = turned(first)
        b = turned(first + 1)
        mat0[pl.ds(i, 75, stride=64), :] = jnp.where(lane75 < shift, a, b) if skip else a
        mat1[pl.ds(i, 75, stride=64), :] = (
            jnp.where(lane75 < shift, b, turned(first + 2)) if skip + edof > 256 else b)

    mat0[count // edof:, :] = jnp.zeros((16, 128), F32)
    mat1[count // edof:, :] = jnp.zeros((16, 128), F32)
    for b in range(2 * nelem):
        rows = slice(b * edof, b * edof + 160)
        ops[b] = jnp.concatenate([mat0[rows, :], mat1[rows, :]], 1).astype(BF)

    for j in range(4):
        @pl.when(has_source(j))
        def _():
            halo_copy(j).wait_recv()

        @pl.when(jnp.logical_not(has_source(j)))
        def _():
            halo_in[j] = jnp.zeros((64, 128), BF)

        half0 = halo_in[j].astype(F32)
        half1 = pltpu.roll(half0, 125, 1)
        for i in range(8):
            at = owned + j * 8
            ext[i, at:at + 8, 0:128] = half0[i * 8:(i + 1) * 8]
            ext[i, at:at + 8, 128:256] = half1[i * 8:(i + 1) * 8]

    lane_face = over_25(iota((1, 256), 1))
    slot_col = jnp.concatenate([jnp.full((nelem, 1), k, jnp.int32) for k in range(6)], 0)
    slot_mask = lane_face == slot_col
    for i in range(8):
        taken = jnp.where(slot_mask, dot_nn(gather, ext[i].astype(BF)), 0.0)
        x = taken[:nelem]
        for k in range(1, 6):
            x = x + taken[k * nelem:(k + 1) * nelem]
        xs0[i * nelem:(i + 1) * nelem, :] = x[:, :128]
        xs1[i * nelem:(i + 1) * nelem, :] = x[:, 128:]

    fill = jnp.zeros((8, 256 - edof), F32)
    for e in range(nelem):
        xa = jnp.concatenate(
            [xs0[pl.ds(e, 8, stride=nelem), :], xs1[pl.ds(e, 8, stride=nelem), :]], 1)
        xb = sign * pltpu.roll(xa, 4, 0)
        y = dot_nt(xa.astype(BF), ops[2 * e]) + dot_nt(xb.astype(BF), ops[2 * e + 1])
        y = y[:, :edof]
        y = jnp.concatenate([y, fill], 1)
        ys0[pl.ds(e, 8, stride=nelem), :] = y[:, :128]
        ys1[pl.ds(e, 8, stride=nelem), :] = y[:, 128:]

    scatter = pick_t.astype(BF)[:ext_rows, :nslot]
    scatter = jnp.concatenate([scatter, scatter], 1)
    summed = []
    for i in range(8):
        rows = slice(i * nelem, (i + 1) * nelem)
        y = jnp.concatenate([ys0[rows, :], ys1[rows, :]], 1)
        y = jnp.where(slot_mask, jnp.concatenate([y] * 6, 0), 0.0)
        high, low = split2(y)
        summed.append(dot_nn(scatter, jnp.concatenate([high, low], 0)))
    fold_lane = iota((1, 128), 1)
    fold = jnp.where((lane_dof == fold_lane), 1.0, 0.0).astype(BF)
    back = jnp.concatenate(
        [s[owned + j * 8:owned + (j + 1) * 8] for j in range(4) for s in summed], 0)
    high, low = split2(back)
    back = dot_nn(high, fold) + dot_nn(low, fold)
    for j in range(4):
        ret_out[j] = back[j * 64:(j + 1) * 64]

        @pl.when(has_source(j))
        def _():
            ret_copy(j).start()

    def rest_wait(i):
        rest_copy(i, peer(i)).wait_recv()

    loop(nall - 1, rest_wait)
    cinv_copy(1 - rep).wait_recv()
    rest_all = jnp.concatenate(
        [rest_in[2 * p] + rest_in[2 * p + 1] for p in range(nall // 2)], 1).astype(BF)
    w = dot_nt(rest_all, cfull[...].reshape(128, rest_all.shape[1]))
    w = w + sign * pltpu.roll(pltpu.roll(w, 96, 1), 4, 0)
    lane128 = iota((8, 128), 1)
    co = jnp.where(lane128 < 32, w, pltpu.roll(w, 96, 1))[:, :64].astype(BF)
    basis = basis_ref[...]
    coarse = dot_nn(co, basis[0]) + sign * pltpu.roll(dot_nn(co, basis[1]), 4, 0)

    half = 4 * nelem
    x0, x1, y0, y1 = xs0[...], xs1[...], ys0[...], ys1[...]
    part_re = x0 * y0 + x1 * y1
    part_im = x0 * pltpu.roll(y0, half, 0) + x1 * pltpu.roll(y1, half, 0)
    part_re = jnp.sum(part_re.reshape(8, nelem, 128), 1)
    part_im = jnp.sum(part_im.reshape(8, nelem, 128), 1)
    part_re = jnp.sum(part_re, 1, keepdims=True) + jnp.sum(rf * coarse, 1, keepdims=True)
    part_im = jnp.sum(part_im, 1, keepdims=True) + jnp.sum(
        rf * pltpu.roll(coarse, 4, 0), 1, keepdims=True)
    part_im = -sign * part_im
    part_re = jnp.broadcast_to(part_re, (8, 128))
    part_im = jnp.broadcast_to(part_im, (8, 128))
    part_re = part_re + pltpu.roll(part_re, 4, 0)
    part_im = part_im + pltpu.roll(part_im, 4, 0)
    mine = jnp.where(lane128 == 0, part_re, part_im)
    inner_out[...] = mine
    inner_in[pl.ds(me, 1)] = mine[None]
    loop(nall - 1, lambda i: inner_copy(i, me).start())

    def spread(parts, mask, depth):
        for start in range(0, length, 256):
            lanes = slice(start, min(start + 256, length))
            wide = dot_nn(parts[0], v6[0:depth, lanes])
            for part in parts[1:]:
                wide = wide + dot_nn(part, v6[0:depth, lanes])
            rows = mask.shape[0]
            keep = mask[:, lanes]
            total = [
                jnp.sum(jnp.where(keep, wide[i * rows:(i + 1) * rows], 0.0), 0, keepdims=True)
                for i in range(8)]
            yield lanes, jnp.concatenate(total, 0)

    own = jnp.concatenate([part[:owned] for part in summed], 0)
    for lanes, value in spread(split2(own), face_mask, 256):
        out_ref[:, lanes] = value + coarse[:, lanes]

    for j in range(4):
        @pl.when(has_reader(j))
        def _():
            ret_copy(j).wait_recv()

        @pl.when(jnp.logical_not(has_reader(j)))
        def _():
            ret_in[j] = jnp.zeros((64, 128), F32)

    send_mask = send_id.astype(jnp.int32) == trace_face
    got = jnp.concatenate(
        [ret_in[j, i * 8:(i + 1) * 8, :] for i in range(8) for j in range(4)], 0)
    high = got.astype(BF).astype(F32)
    got = (high + pltpu.roll(got - high, FACE_DOF, 1)).astype(BF)
    for lanes, value in spread((got,), send_mask, 128):
        out_ref[:, lanes] = out_ref[:, lanes] + value
    loop(nall - 1, lambda i: inner_copy(i, peer(i)).wait_recv())
    out_ref[:, length:length + 128] = jnp.sum(inner_in[...], 0) * (1.0 / total)

    for j in range(4):
        @pl.when(has_reader(j))
        def _():
            halo_copy(j).wait_send()

        @pl.when(has_source(j))
        def _():
            ret_copy(j).wait_send()

    cinv_copy(rep).wait_send()

    def sent(i):
        rest_copy(i, me).wait_send()
        inner_copy(i, me).wait_send()

    loop(nall - 1, sent)


def deliver(full_ref, out_ref, inner_ref):
    length = out_ref.shape[2]
    out_ref[:, 0, :] = full_ref[0:4, 0:length]
    out_ref[:, 1, :] = full_ref[4:8, 0:length]
    inner_ref[...] = full_ref[0:4, length:length + 128].T[0:2]


def solution(mesh):
    nsub = mesh.shape["sub"]
    ncoarse = mesh.shape["coarse"]
    nall = nsub * ncoarse
    placed = (
        P("rep", None, ("groups", "sub", "coarse")),
        P(("groups", "sub", "coarse"), None),
        P(("groups", "sub", "coarse"), None),
        P(("groups", "sub", "coarse"), None, None),
        P(None, ("groups", "sub", "coarse"), None),
        P(None, ("groups", "sub", "coarse", "rep"), None),
    )

    def on_device(residual, elem_inv, elem_faces, send_faces, coarse_basis, coarse_inv):
        length = residual.shape[2]
        count = elem_inv.shape[1]
        vmem = pl.BlockSpec(memory_space=pltpu.VMEM)
        anywhere = pl.BlockSpec(memory_space=pl.ANY)
        dma = pltpu.SemaphoreType.DMA
        full = pl.pallas_call(
            functools.partial(kernel, nsub, ncoarse, length * nall),
            out_shape=jax.ShapeDtypeStruct((8, length + 128), F32),
            in_specs=[vmem, anywhere, vmem, vmem, vmem, vmem],
            out_specs=vmem,
            scratch_shapes=[
                pltpu.VMEM((1, count), BF),
                pltpu.VMEM((count // 128 + 7, 128), F32),
                pltpu.VMEM((count // 150 + 16, 128), F32),
                pltpu.VMEM((count // 150 + 16, 128), F32),
                pltpu.VMEM((2 * elem_faces.shape[0], 160, 256), BF),
                pltpu.VMEM((256, length), BF),
                pltpu.VMEM((8, 80, 256), F32),
                pltpu.VMEM((128, 128), F32),
                pltpu.VMEM((128, 128), F32),
                pltpu.VMEM((128, 128), F32),
                pltpu.VMEM((128, 128), F32),
                pltpu.VMEM((4, 64, 128), BF),
                pltpu.VMEM((4, 64, 128), BF),
                pltpu.VMEM((8, 128), F32),
                pltpu.VMEM((nall, 8, 128), F32),
                pltpu.VMEM((2,) + coarse_inv.shape, BF),
                pltpu.VMEM((4, 64, 128), F32),
                pltpu.VMEM((4, 64, 128), F32),
                pltpu.VMEM((8, 128), F32),
                pltpu.VMEM((nall, 8, 128), F32),
                dma, dma((4,)), dma((4,)), dma((nall,)), dma((nall,)), dma, dma,
                dma((4,)), dma((4,)), dma((nall,)), dma((nall,)),
            ],
            compiler_params=pltpu.CompilerParams(
                collective_id=0, has_side_effects=True, vmem_limit_bytes=56 << 20),
        )(residual, elem_inv, elem_faces.T, send_faces, coarse_basis, coarse_inv)
        out, inner = pl.pallas_call(
            deliver,
            out_shape=(
                jax.ShapeDtypeStruct(residual.shape, F32),
                jax.ShapeDtypeStruct((2, residual.shape[0]), F32),
            ),
            in_specs=[vmem],
            out_specs=(vmem, vmem),
        )(full)
        return out, inner.T

    return jax.shard_map(
        on_device,
        mesh=mesh,
        in_specs=placed,
        out_specs=(P("rep", None, ("groups", "sub", "coarse")), P(("groups", "rep"), None)),
        check_vma=False,
    )
```

```python
import functools

import jax
import jax.numpy as jnp
from jax import lax
from jax.experimental import pallas as pl
from jax.experimental.pallas import tpu as pltpu
from jax.sharding import PartitionSpec as P

FACE_DOF = 25
OFFSETS = (-2, -1, 1, 2)
BF = jnp.bfloat16
F32 = jnp.float32
MESH = pl.DeviceIdType.MESH


def iota(shape, dim):
    return lax.broadcasted_iota(jnp.int32, shape, dim)


def over_25(index):
    return jnp.floor((index.astype(F32) + 0.5) * (1.0 / FACE_DOF)).astype(jnp.int32)


def dot_nt(left, right):
    return lax.dot_general(left, right, (((1,), (1,)), ((), ())), preferred_element_type=F32)


def dot_nn(left, right):
    return lax.dot_general(left, right, (((1,), (0,)), ((), ())), preferred_element_type=F32)


def split2(values):
    high = values.astype(BF)
    return high, (values - high.astype(F32)).astype(BF)


def loop(count, body):
    if count <= 16:
        for i in range(count):
            body(i)
    else:
        def step(i, carry):
            body(i)
            return carry
        lax.fori_loop(0, count, step, 0)


def kernel(
    nsub, ncoarse, total,
    res_ref, elem_ref, faces_ref, send_ref, basis_from, cinv_ref,
    out_ref,
    basis_ref, flat, rows128, mat0, mat1, ops, v6, ext, xs0, xs1, ys0, ys1,
    halo_out, halo_in, rest_out, rest_in, cfull, ret_out, ret_in, inner_out, inner_in,
    basis_sem, elem_sem, halo_send, halo_recv, rest_send, rest_recv, cinv_send, cinv_recv,
    ret_send, ret_recv, inner_send, inner_recv,
):
    nall = nsub * ncoarse
    length = res_ref.shape[2]
    owned = length // FACE_DOF
    slots = 4 * send_ref.shape[2]
    nelem = faces_ref.shape[1]
    ext_rows = owned + slots
    edof = 6 * FACE_DOF
    nslot = 6 * nelem
    rep = lax.axis_index("rep")
    me = lax.axis_index("sub") * ncoarse + lax.axis_index("coarse")

    elem_copy = pltpu.make_async_copy(elem_ref, flat, elem_sem)
    basis_copy = pltpu.make_async_copy(basis_from, basis_ref, basis_sem)
    basis_copy.start()
    elem_copy.start()

    def where_is(other):
        return {"sub": other // ncoarse, "coarse": lax.rem(other, ncoarse)}

    def peer(i):
        return lax.rem(me + i + 1, nall)

    barrier = pltpu.get_barrier_semaphore()
    loop(nall - 1, lambda i: pl.semaphore_signal(
        barrier, inc=1, device_id=where_is(peer(i)), device_id_type=MESH))
    pl.semaphore_signal(barrier, inc=1, device_id={"rep": 1 - rep}, device_id_type=MESH)

    rb = jnp.concatenate([res_ref[:, 0, :], res_ref[:, 1, :]], 0).astype(BF)
    rf = rb.astype(F32)
    sign = jnp.where(iota((8, 1), 0) < 4, -1.0, 1.0).astype(F32)

    trace = iota((1, length), 1)
    trace_face = over_25(trace)
    trace_dof = trace - FACE_DOF * trace_face
    face_mask = iota((owned, length), 0) == trace_face
    face_bf = jnp.where(face_mask, 1.0, 0.0).astype(BF)
    lane_col = iota((256, 1), 0)
    lane_dof = jnp.where(lane_col < edof, lane_col - FACE_DOF * over_25(lane_col), -1)
    v6[...] = jnp.where(lane_dof == trace_dof, 1.0, 0.0).astype(BF)

    id_row = jnp.concatenate(
        [faces_ref[k:k + 1, :] for k in range(6)] + [send_ref[0, j:j + 1, :] for j in range(4)], 1)
    pick_t = jnp.where(iota((128, 128), 0) == id_row, 1.0, 0.0).astype(F32)
    pick = pick_t.T
    send_id = jnp.sum(pick[nslot:] * (iota((slots, 128), 1) + 1).astype(F32), 1, keepdims=True) - 1.0
    pick_b = pick.astype(BF)
    gather = pick_b[:nslot, :ext_rows]
    packer = pick_b[nslot:, :owned]

    left = jnp.concatenate([face_bf * rb[i:i + 1, :] for i in range(8)], 0)
    tiled = dot_nt(left, v6[...])
    packed = []
    for i in range(8):
        part = tiled[i * owned:(i + 1) * owned]
        ext[i, 0:owned, :] = part
        packed.append(dot_nn(packer, part[:, :128].astype(BF)))
    for j in range(4):
        halo_out[j] = jnp.concatenate([part[j * 8:(j + 1) * 8] for part in packed], 0).astype(BF)

    pl.semaphore_wait(barrier, nall)

    def halo_copy(j):
        return pltpu.make_async_remote_copy(
            src_ref=halo_out.at[j], dst_ref=halo_in.at[j], send_sem=halo_send.at[j],
            recv_sem=halo_recv.at[j], device_id=where_is(jnp.clip(me - OFFSETS[j], 0, nall - 1)),
            device_id_type=MESH)

    def ret_copy(j):
        return pltpu.make_async_remote_copy(
            src_ref=ret_out.at[j], dst_ref=ret_in.at[j], send_sem=ret_send.at[j],
            recv_sem=ret_recv.at[j], device_id=where_is(jnp.clip(me + OFFSETS[j], 0, nall - 1)),
            device_id_type=MESH)

    def rest_copy(i, block):
        return pltpu.make_async_remote_copy(
            src_ref=rest_out, dst_ref=rest_in.at[block], send_sem=rest_send.at[i],
            recv_sem=rest_recv.at[block], device_id=where_is(peer(i)), device_id_type=MESH)

    def inner_copy(i, block):
        return pltpu.make_async_remote_copy(
            src_ref=inner_out, dst_ref=inner_in.at[block], send_sem=inner_send.at[i],
            recv_sem=inner_recv.at[block], device_id=where_is(peer(i)), device_id_type=MESH)

    def cinv_copy(half):
        return pltpu.make_async_remote_copy(
            src_ref=cinv_ref, dst_ref=cfull.at[half], send_sem=cinv_send,
            recv_sem=cinv_recv, device_id={"rep": 1 - rep}, device_id_type=MESH)

    def has_reader(j):
        return (me - OFFSETS[j] >= 0) & (me - OFFSETS[j] < nall)

    def has_source(j):
        return (me + OFFSETS[j] >= 0) & (me + OFFSETS[j] < nall)

    for j in range(4):
        @pl.when(has_reader(j))
        def _():
            halo_copy(j).start()

    cinv_copy(rep).start()
    basis_copy.wait()
    basis = basis_ref[...].reshape(128, length)
    q = dot_nt(rb, basis)
    rest = q + sign * pltpu.roll(pltpu.roll(q, 64, 1), 4, 0)
    rest = jnp.where(iota((8, 128), 1) < 64, rest.astype(BF).astype(F32), 0.0)
    rest = jnp.where(lax.rem(me, 2) == 1, pltpu.roll(rest, 64, 1), rest)
    rest_out[...] = rest
    rest_in[pl.ds(me, 1)] = rest[None]

    loop(nall - 1, lambda i: rest_copy(i, me).start())
    cfull[pl.ds(rep, 1)] = cinv_ref[...][None]

    elem_copy.wait()
    count = flat.shape[1]
    nrows = count // 128
    full = nrows // 64

    def widen(i, carry):
        start = pl.multiple_of(i * 8192, 8192)
        to = pl.multiple_of(i * 64, 64)
        rows128[pl.ds(to, 64), :] = flat[0:1, pl.ds(start, 8192)].astype(F32).reshape(64, 128)
        return carry

    lax.fori_loop(0, full, widen, 0, unroll=3)
    rest_rows = nrows - full * 64
    rows128[full * 64:nrows, :] = flat[0:1, full * 8192:count].astype(F32).reshape(rest_rows, 128)
    lane75 = iota((75, 128), 1)
    for i in range(64):
        first = (edof * i) // 128
        skip = edof * i - 128 * first
        shift = 128 - skip

        def turned(row):
            block = rows128[pl.ds(row, 75, stride=75), :]
            return pltpu.roll(block, shift, 1) if skip else block

        a = turned(first)
        b = turned(first + 1)
        mat0[pl.ds(i, 75, stride=64), :] = jnp.where(lane75 < shift, a, b) if skip else a
        mat1[pl.ds(i, 75, stride=64), :] = (
            jnp.where(lane75 < shift, b, turned(first + 2)) if skip + edof > 256 else b)

    mat0[count // edof:, :] = jnp.zeros((16, 128), F32)
    mat1[count // edof:, :] = jnp.zeros((16, 128), F32)
    for b in range(2 * nelem):
        rows = slice(b * edof, b * edof + 160)
        ops[b] = jnp.concatenate([mat0[rows, :], mat1[rows, :]], 1).astype(BF)

    for j in range(4):
        @pl.when(has_source(j))
        def _():
            halo_copy(j).wait_recv()

        @pl.when(jnp.logical_not(has_source(j)))
        def _():
            halo_in[j] = jnp.zeros((64, 128), BF)

        half0 = halo_in[j].astype(F32)
        half1 = pltpu.roll(half0, 125, 1)
        for i in range(8):
            at = owned + j * 8
            ext[i, at:at + 8, 0:128] = half0[i * 8:(i + 1) * 8]
            ext[i, at:at + 8, 128:256] = half1[i * 8:(i + 1) * 8]

    lane_face = over_25(iota((1, 256), 1))
    slot_col = jnp.concatenate([jnp.full((nelem, 1), k, jnp.int32) for k in range(6)], 0)
    slot_mask = lane_face == slot_col
    for i in range(8):
        taken = jnp.where(slot_mask, dot_nn(gather, ext[i].astype(BF)), 0.0)
        x = taken[:nelem]
        for k in range(1, 6):
            x = x + taken[k * nelem:(k + 1) * nelem]
        xs0[i * nelem:(i + 1) * nelem, :] = x[:, :128]
        xs1[i * nelem:(i + 1) * nelem, :] = x[:, 128:]

    fill = jnp.zeros((8, 256 - edof), F32)
    for e in range(nelem):
        xa = jnp.concatenate(
            [xs0[pl.ds(e, 8, stride=nelem), :], xs1[pl.ds(e, 8, stride=nelem), :]], 1)
        xb = sign * pltpu.roll(xa, 4, 0)
        y = dot_nt(xa.astype(BF), ops[2 * e]) + dot_nt(xb.astype(BF), ops[2 * e + 1])
        y = y[:, :edof]
        y = jnp.concatenate([y, fill], 1)
        ys0[pl.ds(e, 8, stride=nelem), :] = y[:, :128]
        ys1[pl.ds(e, 8, stride=nelem), :] = y[:, 128:]

    scatter = pick_t.astype(BF)[:ext_rows, :nslot]
    scatter = jnp.concatenate([scatter, scatter], 1)
    summed = []
    for i in range(8):
        rows = slice(i * nelem, (i + 1) * nelem)
        y = jnp.concatenate([ys0[rows, :], ys1[rows, :]], 1)
        y = jnp.where(slot_mask, jnp.concatenate([y] * 6, 0), 0.0)
        high, low = split2(y)
        summed.append(dot_nn(scatter, jnp.concatenate([high, low], 0)))
    fold_lane = iota((1, 128), 1)
    fold = jnp.where((lane_dof == fold_lane), 1.0, 0.0).astype(BF)
    back = jnp.concatenate(
        [s[owned + j * 8:owned + (j + 1) * 8] for j in range(4) for s in summed], 0)
    high, low = split2(back)
    back = dot_nn(high, fold) + dot_nn(low, fold)
    for j in range(4):
        ret_out[j] = back[j * 64:(j + 1) * 64]

        @pl.when(has_source(j))
        def _():
            ret_copy(j).start()

    def rest_wait(i):
        rest_copy(i, peer(i)).wait_recv()

    loop(nall - 1, rest_wait)
    cinv_copy(1 - rep).wait_recv()
    rest_all = jnp.concatenate(
        [rest_in[2 * p] + rest_in[2 * p + 1] for p in range(nall // 2)], 1).astype(BF)
    w = dot_nt(rest_all, cfull[...].reshape(128, rest_all.shape[1]))
    w = w + sign * pltpu.roll(pltpu.roll(w, 96, 1), 4, 0)
    lane128 = iota((8, 128), 1)
    co = jnp.where(lane128 < 32, w, pltpu.roll(w, 96, 1))[:, :64].astype(BF)
    basis = basis_ref[...]
    coarse = dot_nn(co, basis[0]) + sign * pltpu.roll(dot_nn(co, basis[1]), 4, 0)

    half = 4 * nelem
    x0, x1, y0, y1 = xs0[...], xs1[...], ys0[...], ys1[...]
    part_re = x0 * y0 + x1 * y1
    part_im = x0 * pltpu.roll(y0, half, 0) + x1 * pltpu.roll(y1, half, 0)
    part_re = jnp.sum(part_re.reshape(8, nelem, 128), 1)
    part_im = jnp.sum(part_im.reshape(8, nelem, 128), 1)
    part_re = jnp.sum(part_re, 1, keepdims=True) + jnp.sum(rf * coarse, 1, keepdims=True)
    part_im = jnp.sum(part_im, 1, keepdims=True) + jnp.sum(
        rf * pltpu.roll(coarse, 4, 0), 1, keepdims=True)
    part_im = -sign * part_im
    part_re = jnp.broadcast_to(part_re, (8, 128))
    part_im = jnp.broadcast_to(part_im, (8, 128))
    part_re = part_re + pltpu.roll(part_re, 4, 0)
    part_im = part_im + pltpu.roll(part_im, 4, 0)
    mine = jnp.where(lane128 == 0, part_re, part_im)
    inner_out[...] = mine
    inner_in[pl.ds(me, 1)] = mine[None]
    loop(nall - 1, lambda i: inner_copy(i, me).start())

    def spread(parts, mask, depth):
        for start in range(0, length, 256):
            lanes = slice(start, min(start + 256, length))
            wide = dot_nn(parts[0], v6[0:depth, lanes])
            for part in parts[1:]:
                wide = wide + dot_nn(part, v6[0:depth, lanes])
            rows = mask.shape[0]
            keep = mask[:, lanes]
            total = [
                jnp.sum(jnp.where(keep, wide[i * rows:(i + 1) * rows], 0.0), 0, keepdims=True)
                for i in range(8)]
            yield lanes, jnp.concatenate(total, 0)

    own = jnp.concatenate([part[:owned] for part in summed], 0)
    for lanes, value in spread(split2(own), face_mask, 256):
        out_ref[:, lanes] = value + coarse[:, lanes]

    for j in range(4):
        @pl.when(has_reader(j))
        def _():
            ret_copy(j).wait_recv()

        @pl.when(jnp.logical_not(has_reader(j)))
        def _():
            ret_in[j] = jnp.zeros((64, 128), F32)

    send_mask = send_id.astype(jnp.int32) == trace_face
    got = jnp.concatenate(
        [ret_in[j, i * 8:(i + 1) * 8, :] for i in range(8) for j in range(4)], 0)
    high = got.astype(BF).astype(F32)
    got = (high + pltpu.roll(got - high, FACE_DOF, 1)).astype(BF)
    for lanes, value in spread((got,), send_mask, 128):
        out_ref[:, lanes] = out_ref[:, lanes] + value
    loop(nall - 1, lambda i: inner_copy(i, peer(i)).wait_recv())
    out_ref[:, length:length + 128] = jnp.sum(inner_in[...], 0) * (1.0 / total)

    for j in range(4):
        @pl.when(has_reader(j))
        def _():
            halo_copy(j).wait_send()

        @pl.when(has_source(j))
        def _():
            ret_copy(j).wait_send()

    cinv_copy(rep).wait_send()

    def sent(i):
        rest_copy(i, me).wait_send()
        inner_copy(i, me).wait_send()

    loop(nall - 1, sent)


def deliver(full_ref, out_ref, inner_ref):
    length = out_ref.shape[2]
    out_ref[:, 0, :] = full_ref[0:4, 0:length]
    out_ref[:, 1, :] = full_ref[4:8, 0:length]
    inner_ref[...] = full_ref[0:4, length:length + 128].T[0:2]


def solution(mesh):
    nsub = mesh.shape["sub"]
    ncoarse = mesh.shape["coarse"]
    nall = nsub * ncoarse
    placed = (
        P("rep", None, ("groups", "sub", "coarse")),
        P(("groups", "sub", "coarse"), None),
        P(("groups", "sub", "coarse"), None),
        P(("groups", "sub", "coarse"), None, None),
        P(None, ("groups", "sub", "coarse"), None),
        P(None, ("groups", "sub", "coarse", "rep"), None),
    )

    def on_device(residual, elem_inv, elem_faces, send_faces, coarse_basis, coarse_inv):
        length = residual.shape[2]
        count = elem_inv.shape[1]
        vmem = pl.BlockSpec(memory_space=pltpu.VMEM)
        anywhere = pl.BlockSpec(memory_space=pl.ANY)
        dma = pltpu.SemaphoreType.DMA
        full = pl.pallas_call(
            functools.partial(kernel, nsub, ncoarse, length * nall),
            out_shape=jax.ShapeDtypeStruct((8, length + 128), F32),
            in_specs=[vmem, anywhere, vmem, vmem, anywhere, vmem],
            out_specs=vmem,
            scratch_shapes=[
                pltpu.VMEM(coarse_basis.shape, BF),
                pltpu.VMEM((1, count), BF),
                pltpu.VMEM((count // 128 + 7, 128), F32),
                pltpu.VMEM((count // 150 + 16, 128), F32),
                pltpu.VMEM((count // 150 + 16, 128), F32),
                pltpu.VMEM((2 * elem_faces.shape[0], 160, 256), BF),
                pltpu.VMEM((256, length), BF),
                pltpu.VMEM((8, 80, 256), F32),
                pltpu.VMEM((128, 128), F32),
                pltpu.VMEM((128, 128), F32),
                pltpu.VMEM((128, 128), F32),
                pltpu.VMEM((128, 128), F32),
                pltpu.VMEM((4, 64, 128), BF),
                pltpu.VMEM((4, 64, 128), BF),
                pltpu.VMEM((8, 128), F32),
                pltpu.VMEM((nall, 8, 128), F32),
                pltpu.VMEM((2,) + coarse_inv.shape, BF),
                pltpu.VMEM((4, 64, 128), F32),
                pltpu.VMEM((4, 64, 128), F32),
                pltpu.VMEM((8, 128), F32),
                pltpu.VMEM((nall, 8, 128), F32),
                dma, dma, dma((4,)), dma((4,)), dma((nall,)), dma((nall,)), dma, dma,
                dma((4,)), dma((4,)), dma((nall,)), dma((nall,)),
            ],
            compiler_params=pltpu.CompilerParams(
                collective_id=0, has_side_effects=True, vmem_limit_bytes=56 << 20),
        )(residual, elem_inv, elem_faces.T, send_faces, coarse_basis, coarse_inv)
        out, inner = pl.pallas_call(
            deliver,
            out_shape=(
                jax.ShapeDtypeStruct(residual.shape, F32),
                jax.ShapeDtypeStruct((2, residual.shape[0]), F32),
            ),
            in_specs=[vmem],
            out_specs=(vmem, vmem),
        )(full)
        return out, inner.T

    return jax.shard_map(
        on_device,
        mesh=mesh,
        in_specs=placed,
        out_specs=(P("rep", None, ("groups", "sub", "coarse")), P(("groups", "rep"), None)),
        check_vma=False,
    )
```
